256 devices in a mesh: blk: 64 (over x_hi, y, z), col: 4 (over x_lo, core).
Axes of the slice: x: 4 (x_hi: 2, x_lo: 2; x = x_hi * 2 + x_lo), y: 4, z: 8, core: 2. Of those that a mesh axis runs over, the one named last changes fastest.
Arguments:
- amplitudes: bfloat16 [12288, 8192], P('blk', 'col'), may hold values from -6 to 6
- integrals: bfloat16 [65536, 8192], P('blk', 'col'), may hold values from -0.0625 to 0.0625
- allowed: int32 [8, 8, 8], replicated, may hold values 0 or 1
- partner: int32 [8, 1536], replicated, may hold values from 0 to 1535, as said below
Outputs:
- residual: bfloat16 [1536, 65536], P('col', 'blk')
The draws below stay inside these ranges and needn't reach their ends.
Inputs may be any that keep to these rules, and one draw needn't show every extreme that they name: partner[s, partner[s, p]] = p and partner[s, p] != p for every s and p.
All inputs are finite; a program needn't handle non-finite values.
Results may differ from the reference program's by a relative error of at most 0.001.
Values may be sent and summed in bfloat16 or wider, within the bound.
A program may use at most 128 MiB of HBM per device.

```python
import jax
import jax.numpy as jnp
from jax import lax

NB = 8
PAIRS = 1536
TW = 1024
VPAIRS = 8192
SECTORS = 8


def draw_partner(key, part):
    key = jax.random.fold_in(key, 7)
    sector_keys = jax.random.split(key, SECTORS)

    def pair_up(sector_key):
        shuffled = jax.random.permutation(sector_key, PAIRS).astype(jnp.int32)
        swapped = shuffled.reshape(PAIRS // 2, 2)[:, ::-1].reshape(PAIRS)
        return jnp.zeros((PAIRS,), jnp.int32).at[shuffled].set(swapped)
    return jax.vmap(pair_up)(sector_keys)


def with_ends(array, rng, smallest, largest):
    extent = array.shape
    index_at = [jax.random.randint(jax.random.fold_in(rng, axis), (), 0, extent[axis]) for axis in range(len(extent))]
    array = array.at[tuple(index_at)].set(smallest)
    longest = extent.index(max(extent))
    index_at[longest] = (index_at[longest] + 1) % extent[longest]
    return array.at[tuple(index_at)].set(largest)


def levels(own_key, dims, cuts, least, top_value):
    def one(axis_at, blocks):
        steps = jax.random.uniform(jax.random.fold_in(jax.random.fold_in(own_key, 6), axis_at), (blocks,), jnp.float32, least / len(cuts), top_value / len(cuts))
        return jnp.repeat(jnp.exp(steps), dims[axis_at] // blocks).reshape((-1,) + (1,) * (len(dims) - axis_at - 1))

    factor_of = one(*cuts[0])
    for cut in cuts[1:]:
        factor_of = factor_of * one(*cut)
    return factor_of


def gaussian(stream_key, extent, spread, most, cuts=(), kind=jnp.bfloat16):
    level = levels(stream_key, extent, cuts, -0.22, 0.18) if cuts else 1.0
    array = jax.random.normal(stream_key, extent, jnp.float32) * spread * level
    return jnp.minimum(jnp.maximum(array, -most), most).astype(kind)


def setup_inputs(seed: int = 0) -> dict:
    streams_of = jax.random.split(jax.random.key(seed), 5)
    return {
        "amplitudes": gaussian(streams_of[0], (SECTORS * PAIRS, VPAIRS), 1.0, 6.0, ((0, 64), (1, 4))),
        "integrals": gaussian(streams_of[1], (SECTORS * VPAIRS, VPAIRS), VPAIRS ** -0.5, 0.0625, ((0, 64), (1, 4))),
        "allowed": with_ends((jax.random.randint(streams_of[2], (SECTORS, NB, NB), 0, 8) < 5).astype(jnp.int32), jax.random.fold_in(streams_of[2], 1), 0, 1),
        "partner": draw_partner(jax.random.fold_in(streams_of[4], 71), 0),
    }


def reference(amplitudes, integrals, allowed, partner):
    def per_sector(sector):
        rows_amp = lax.dynamic_slice_in_dim(amplitudes, sector * PAIRS, PAIRS, 0)
        rows_int = lax.dynamic_slice_in_dim(integrals, sector * VPAIRS, VPAIRS, 0)
        sector_grid = lax.dynamic_index_in_dim(allowed, sector, 0, keepdims=False)
        blocked = rows_int.reshape(NB, TW, NB, TW) * sector_grid.astype(rows_int.dtype)[:, None, :, None]
        masked = blocked.reshape(VPAIRS, VPAIRS)
        ladder = jnp.dot(rows_amp, masked.T, preferred_element_type=jnp.float32)
        pair_rows = lax.dynamic_index_in_dim(partner, sector, 0, keepdims=False)
        mirrored = jnp.take(ladder, pair_rows, axis=0)
        return (0.5 * (ladder - mirrored)).astype(jnp.bfloat16)

    stacked = lax.map(per_sector, jnp.arange(SECTORS, dtype=jnp.int32))
    return jnp.transpose(stacked, (1, 0, 2)).reshape(PAIRS, SECTORS * VPAIRS)
```

```python
import functools

import jax
import jax.numpy as jnp
from jax import lax
from jax.experimental import pallas as pl
from jax.experimental.pallas import tpu as pltpu
from jax.sharding import PartitionSpec as P

MESH = pl.DeviceIdType.MESH
RING = 8
PIECES = 4
WINDOW = 4
FINAL_CUTS = 2
GROUP = 16


def kernel(
    amplitudes, integrals, allowed, partner, out,
    held, weights, own, to_core, from_core, to_x, from_x, ladder, mirror, finished,
    load_sem, ring_send, ring_recv, core_send, core_recv, x_send, x_recv, final_send, final_recv, local_sem,
):
    pieces, piece_rows, depth = amplitudes.shape
    half = pieces // 2
    arrivals = pieces * (RING - 1) // 2
    steps = half + arrivals
    block_rows = pieces * piece_rows
    quarter = integrals.shape[0] // 4
    out_rows = out.shape[0]

    blk, col = lax.axis_index("blk"), lax.axis_index("col")
    sector, member = blk // RING, blk % RING
    side, core = col // 2, col % 2
    first = sector * RING
    right = (first + (member + 1) % RING, col)
    left = (first + (member + RING - 1) % RING, col)
    core_peer = (blk, side * 2 + 1 - core)
    x_peer = (blk, (1 - side) * 2 + core)
    far_peer = (blk, (1 - side) * 2 + 1 - core)

    load_t = pltpu.make_async_copy(amplitudes, held.at[pl.ds(0, pieces)], load_sem.at[0])
    load_v = pltpu.make_async_copy(integrals, weights, load_sem.at[1])
    load_t.start()
    load_v.start()

    barrier = pltpu.get_barrier_semaphore()
    for peer in (right, left, core_peer, x_peer, far_peer):
        pl.semaphore_signal(barrier, inc=1, device_id=peer, device_id_type=MESH)
    pl.semaphore_wait(barrier, 5)

    def ring_copy(way, k, source=None):
        if source is None:
            start = k if way == 0 else (k + half) % pieces
            forward = pieces + 2 * (k - pieces) + way
            source = held.at[jnp.where(k < pieces, start, forward)]
        return pltpu.make_async_remote_copy(
            src_ref=source,
            dst_ref=held.at[pieces + 2 * k + way],
            send_sem=ring_send.at[way, k],
            recv_sem=ring_recv.at[way, k],
            device_id=(right, left)[way],
            device_id_type=MESH,
        )

    def core_copy(s):
        return pltpu.make_async_remote_copy(
            src_ref=to_core.at[s], dst_ref=from_core.at[s], send_sem=core_send.at[s], recv_sem=core_recv.at[s],
            device_id=core_peer, device_id_type=MESH,
        )

    def x_copy(s):
        return pltpu.make_async_remote_copy(
            src_ref=to_x.at[s], dst_ref=from_x.at[s], send_sem=x_send.at[s], recv_sem=x_recv.at[s],
            device_id=x_peer, device_id_type=MESH,
        )

    for k in range(WINDOW):
        ring_copy(0, k, amplitudes.at[k]).start()
        ring_copy(1, k, amplitudes.at[(k + half) % pieces]).start()

    load_v.wait()
    strip = 64
    width = depth // 2
    for tile in range(2):
        flag = allowed[sector, member, col * 2 + tile].astype(jnp.float32)
        factor = jnp.full((strip, width), flag, jnp.float32).astype(jnp.bfloat16)

        def mask(i, carry, tile=tile, factor=factor):
            at = (pl.ds(pl.multiple_of(i * strip, strip), strip), pl.ds(tile * width, width))
            weights[at] = weights[at] * factor
            return carry

        lax.fori_loop(0, integrals.shape[0] // strip, mask, 0)
    load_t.wait()

    def product(s, e_block):
        rows = held[pl.ds(2 * s, 2)].reshape(2 * piece_rows, depth)
        block = weights[pl.ds(pl.multiple_of(e_block * quarter, quarter), quarter), :]
        return lax.dot_general(rows, block, (((1,), (1,)), ((), ())), preferred_element_type=jnp.float32)

    def rows_at(s, way):
        t = s - half
        t_block = jnp.where(way == 0, member + RING - 1 - t // pieces, member + 1 + t // pieces) % RING
        t_piece = jnp.where(way == 0, t % pieces, (t % pieces + half) % pieces)
        block = jnp.where(s < half, member, t_block)
        piece = jnp.where(s < half, 2 * s + way, t_piece)
        return pl.multiple_of(block * block_rows + piece * piece_rows, piece_rows)

    def step(s, carry):
        @pl.when(jnp.logical_and(s >= half, s < steps))
        def _():
            t = s - half
            for way in range(2):
                ring_copy(way, t).wait_recv()

            @pl.when(t + WINDOW < arrivals)
            def _():
                for way in range(2):
                    ring_copy(way, t + WINDOW).start()

        @pl.when(s < steps)
        def _():
            to_core[s, 0] = product(s, (1 - core) * 2 + 1 - side)
            to_core[s, 1] = product(s, (1 - core) * 2 + side)
            core_copy(s).start()
            own[s, 0] = product(s, core * 2 + 1 - side)
            own[s, 1] = product(s, core * 2 + side)

        @pl.when(jnp.logical_and(s >= 1, s < steps + 1))
        def _():
            core_copy(s - 1).wait_recv()
            to_x[s - 1] = own[s - 1, 0] + from_core[s - 1, 0]
            x_copy(s - 1).start()

        @pl.when(s >= 2)
        def _():
            x_copy(s - 2).wait_recv()
            total = own[s - 2, 1] + from_core[s - 2, 1] + from_x[s - 2]
            ladder[pl.ds(rows_at(s - 2, 0), piece_rows), :] = total[:piece_rows]
            ladder[pl.ds(rows_at(s - 2, 1), piece_rows), :] = total[piece_rows:]

        return carry

    lax.fori_loop(0, steps + 2, step, 0)

    cut_rows = out_rows // FINAL_CUTS
    e_start = pl.multiple_of((core * 2 + side) * quarter, quarter)

    def final_copy(turn, cut, peer):
        return pltpu.make_async_remote_copy(
            src_ref=finished.at[turn, pl.ds(cut * cut_rows, cut_rows)],
            dst_ref=out.at[pl.ds(cut * cut_rows, cut_rows), pl.ds(e_start, quarter)],
            send_sem=final_send.at[turn, cut],
            recv_sem=final_recv.at[turn, cut],
            device_id=peer,
            device_id_type=MESH,
        )

    turns = (far_peer, x_peer, core_peer, None)
    for turn, peer in enumerate(turns):
        owner = col if peer is None else peer[1]
        for cut in range(FINAL_CUTS):
            start = owner * out_rows + cut * cut_rows

            def group(g, carry, turn=turn, cut=cut, start=start):
                at = pl.multiple_of(start + g * GROUP, GROUP)
                for i in range(GROUP):
                    mirror[pl.ds(at + i, 1), :] = ladder[pl.ds(partner[sector, at + i], 1), :]
                value = 0.5 * (ladder[pl.ds(at, GROUP), :] - mirror[pl.ds(at, GROUP), :])
                finished[turn, pl.ds(pl.multiple_of(cut * cut_rows + g * GROUP, GROUP), GROUP), :] = value.astype(out.dtype)
                return carry

            lax.fori_loop(0, cut_rows // GROUP, group, 0)
            if peer is not None:
                final_copy(turn, cut, peer).start()
    mine = pltpu.make_async_copy(finished.at[3], out.at[:, pl.ds(e_start, quarter)], local_sem)
    mine.start()

    for turn, peer in enumerate(turns[:3]):
        for cut in range(FINAL_CUTS):
            final_copy(turn, cut, peer).wait()
    mine.wait()

    def drain_ring(k, carry):
        for way in range(2):
            ring_copy(way, k).wait_send()
        return carry

    def drain_sums(s, carry):
        core_copy(s).wait_send()
        x_copy(s).wait_send()
        return carry

    lax.fori_loop(0, arrivals, drain_ring, 0)
    lax.fori_loop(0, steps, drain_sums, 0)


def body(amplitudes, integrals, allowed, partner):
    rows, depth = amplitudes.shape
    e_rows = integrals.shape[0]
    pieces, piece_rows, quarter = PIECES, rows // PIECES, e_rows // 4
    arrivals = pieces * (RING - 1) // 2
    steps = pieces // 2 + arrivals
    pairs = rows * RING
    out_rows = pairs // 4
    f32, bf16 = jnp.float32, jnp.bfloat16
    dma = pltpu.SemaphoreType.DMA
    anywhere = pl.BlockSpec(memory_space=pl.ANY)
    scalars = pl.BlockSpec(memory_space=pltpu.SMEM)
    return pl.pallas_call(
        kernel,
        out_shape=jax.ShapeDtypeStruct((out_rows, e_rows), bf16),
        in_specs=[anywhere, anywhere, scalars, scalars],
        out_specs=anywhere,
        scratch_shapes=[
            pltpu.VMEM((RING * pieces, piece_rows, depth), bf16),
            pltpu.VMEM((e_rows, depth), bf16),
            pltpu.VMEM((steps, 2, 2 * piece_rows, quarter), f32),
            pltpu.VMEM((steps, 2, 2 * piece_rows, quarter), f32),
            pltpu.VMEM((steps, 2, 2 * piece_rows, quarter), f32),
            pltpu.VMEM((steps, 2 * piece_rows, quarter), f32),
            pltpu.VMEM((steps, 2 * piece_rows, quarter), f32),
            pltpu.VMEM((pairs, quarter), f32),
            pltpu.VMEM((pairs, quarter), f32),
            pltpu.VMEM((4, out_rows, quarter), bf16),
            dma((2,)),
            dma((2, arrivals)),
            dma((2, arrivals)),
            dma((steps,)),
            dma((steps,)),
            dma((steps,)),
            dma((steps,)),
            dma((3, FINAL_CUTS)),
            dma((3, FINAL_CUTS)),
            dma(()),
        ],
        compiler_params=pltpu.CompilerParams(
            collective_id=0, has_side_effects=True, vmem_limit_bytes=48 * 1024 * 1024
        ),
        cost_estimate=pl.CostEstimate(
            flops=2 * pairs * e_rows * depth, bytes_accessed=2 * (e_rows * depth + rows * depth + out_rows * e_rows), transcendentals=0
        ),
        name="ladder_residual",
    )(amplitudes.reshape(pieces, piece_rows, depth), integrals, allowed, partner)


def solution(mesh):
    return jax.shard_map(
        body,
        mesh=mesh,
        in_specs=(P("blk", "col"), P("blk", "col"), P(), P()),
        out_specs=P("col", "blk"),
        check_vma=False,
    )
```

```python
import functools

import jax
import jax.numpy as jnp
from jax import lax
from jax.experimental import pallas as pl
from jax.experimental.pallas import tpu as pltpu
from jax.sharding import PartitionSpec as P

MESH = pl.DeviceIdType.MESH
RING = 8
PIECES = 4
WINDOW = 4
FINAL_CUTS = 4
GROUP = 16
LANES = 128
SUM_LAG, PASS_LAG, PICK_LAG = 1, 3, 4


def kernel(
    amplitudes, integrals, allowed_in, partner_in, out,
    allowed, partner, held, weights, own, to_core, from_core, to_x, from_x, ladder, mirror, results, partners, chosen, rounded,
    load_sem, ring_send, ring_recv, core_send, core_recv, x_send, x_recv, row_send, row_recv, out_sem,
):
    pieces, piece_rows, depth = amplitudes.shape
    half = pieces // 2
    arrivals = pieces * (RING - 1) // 2
    steps = half + arrivals
    block_rows = pieces * piece_rows
    quarter = integrals.shape[0] // 4
    out_rows = out.shape[0]

    blk, col = lax.axis_index("blk"), lax.axis_index("col")
    sector, member = blk // RING, blk % RING
    side, core = col // 2, col % 2
    first = sector * RING
    right = (first + (member + 1) % RING, col)
    left = (first + (member + RING - 1) % RING, col)
    core_peer = (blk, side * 2 + 1 - core)
    x_peer = (blk, (1 - side) * 2 + core)

    load_t = pltpu.make_async_copy(amplitudes, held.at[pl.ds(0, pieces)], load_sem.at[0])
    load_v = pltpu.make_async_copy(integrals, weights, load_sem.at[1])
    load_allowed = pltpu.make_async_copy(allowed_in, allowed, load_sem.at[2])
    load_partner = pltpu.make_async_copy(partner_in, partner, load_sem.at[3])
    load_t.start()
    load_v.start()
    load_allowed.start()
    load_partner.start()

    barrier = pltpu.get_barrier_semaphore()
    for peer in (right, left, core_peer, x_peer):
        pl.semaphore_signal(barrier, inc=1, device_id=peer, device_id_type=MESH)
    pl.semaphore_wait(barrier, 4)

    def ring_copy(way, k, source=None):
        if source is None:
            start = k if way == 0 else (k + half) % pieces
            forward = pieces + 2 * (k - pieces) + way
            source = held.at[jnp.where(k < pieces, start, forward)]
        return pltpu.make_async_remote_copy(
            src_ref=source,
            dst_ref=held.at[pieces + 2 * k + way],
            send_sem=ring_send.at[way, k],
            recv_sem=ring_recv.at[way, k],
            device_id=(right, left)[way],
            device_id_type=MESH,
        )

    def row_copy(kind, s):
        place = results.at[s, core * 2 + (1 - side if kind == 2 else side)]
        return pltpu.make_async_remote_copy(
            src_ref=place, dst_ref=place, send_sem=row_send.at[kind, s], recv_sem=row_recv.at[kind, s],
            device_id=x_peer if kind == 0 else core_peer, device_id_type=MESH,
        )

    def core_copy(s):
        return pltpu.make_async_remote_copy(
            src_ref=to_core.at[s], dst_ref=from_core.at[s], send_sem=core_send.at[s], recv_sem=core_recv.at[s],
            device_id=core_peer, device_id_type=MESH,
        )

    def x_copy(s):
        return pltpu.make_async_remote_copy(
            src_ref=to_x.at[s], dst_ref=from_x.at[s], send_sem=x_send.at[s], recv_sem=x_recv.at[s],
            device_id=x_peer, device_id_type=MESH,
        )

    for k in range(WINDOW):
        ring_copy(0, k, amplitudes.at[k]).start()
        ring_copy(1, k, amplitudes.at[(k + half) % pieces]).start()

    ladder[...] = jnp.zeros_like(ladder)
    load_partner.wait()

    def spread(g, carry):
        for i in range(GROUP):
            value = partner[sector, col * out_rows + g * GROUP + i]
            partners[pl.ds(g * GROUP + i, 1), :] = jnp.full((1, LANES), value, jnp.int32)
        return carry

    lax.fori_loop(0, out_rows // GROUP, spread, 0)
    load_allowed.wait()
    load_v.wait()
    strip = 64
    width = depth // 2
    for tile in range(2):
        flag = allowed[sector, member, col * 2 + tile].astype(jnp.float32)
        factor = jnp.full((strip, width), flag, jnp.float32).astype(jnp.bfloat16)

        def mask(i, carry, tile=tile, factor=factor):
            at = (pl.ds(pl.multiple_of(i * strip, strip), strip), pl.ds(tile * width, width))
            weights[at] = weights[at] * factor
            return carry

        lax.fori_loop(0, integrals.shape[0] // strip, mask, 0)
    load_t.wait()

    def product(s, e_block):
        rows = held[pl.ds(2 * s, 2)].reshape(2 * piece_rows, depth)
        block = weights[pl.ds(pl.multiple_of(e_block * quarter, quarter), quarter), :]
        return lax.dot_general(rows, block, (((1,), (1,)), ((), ())), preferred_element_type=jnp.float32)

    def rows_at(s, way):
        t = s - half
        t_block = jnp.where(way == 0, member + RING - 1 - t // pieces, member + 1 + t // pieces) % RING
        t_piece = jnp.where(way == 0, t % pieces, (t % pieces + half) % pieces)
        block = jnp.where(s < half, member, t_block)
        piece = jnp.where(s < half, 2 * s + way, t_piece)
        return pl.multiple_of(block * block_rows + piece * piece_rows, piece_rows)

    def in_chunk(rows, s):
        first_rows, second_rows = rows_at(s, 0), rows_at(s, 1)
        return jnp.logical_or(
            jnp.logical_and(rows >= first_rows, rows < first_rows + piece_rows),
            jnp.logical_and(rows >= second_rows, rows < second_rows + piece_rows),
        )

    def pick(s):
        shape = (out_rows, 2 * piece_rows)
        mine = col * out_rows + lax.broadcasted_iota(jnp.int32, shape, 0)
        other = partners[:, : 2 * piece_rows]
        lane = lax.broadcasted_iota(jnp.int32, shape, 1)
        at_lane = jnp.where(lane < piece_rows, rows_at(s, 0) + lane, rows_at(s, 1) + lane - piece_rows)
        mine_here = in_chunk(mine, s)
        wanted = jnp.where(mine_here, mine, other)
        sign = jnp.where(mine_here, 1.0, -1.0)
        choice = jnp.where(wanted == at_lane, sign, 0.0).astype(jnp.bfloat16)
        mine_wide = col * out_rows + lax.broadcasted_iota(jnp.int32, (out_rows, LANES), 0)
        hit = jnp.logical_or(in_chunk(mine_wide, s), in_chunk(partners[...], s))
        for e_block in range(4):
            fresh = jnp.dot(choice, results[s, e_block], preferred_element_type=jnp.float32)
            for lanes in range(0, quarter, LANES):
                at = slice(e_block * quarter + lanes, e_block * quarter + lanes + LANES)
                chosen[:, at] = jnp.where(hit, fresh[:, lanes : lanes + LANES], chosen[:, at])

    def drain_ring(k, carry):
        for way in range(2):
            ring_copy(way, k).wait_send()
        return carry

    def drain_sums(s, carry):
        core_copy(s).wait_send()
        x_copy(s).wait_send()
        return carry

    def drain_rows(s, carry):
        for kind in range(3):
            row_copy(kind, s).wait_send()
        return carry

    def step(s, carry):
        @pl.when(jnp.logical_and(s >= half, s < steps))
        def _():
            t = s - half
            for way in range(2):
                ring_copy(way, t).wait_recv()

            @pl.when(t + WINDOW < arrivals)
            def _():
                for way in range(2):
                    ring_copy(way, t + WINDOW).start()

        @pl.when(s < steps)
        def _():
            to_core[s, 0] = product(s, (1 - core) * 2 + 1 - side)
            to_core[s, 1] = product(s, (1 - core) * 2 + side)
            core_copy(s).start()
            own[s, 0] = product(s, core * 2 + 1 - side)
            own[s, 1] = product(s, core * 2 + side)

        @pl.when(jnp.logical_and(s >= PASS_LAG, s < steps + PASS_LAG))
        def _():
            row_copy(0, s - PASS_LAG).wait_recv()
            row_copy(2, s - PASS_LAG).start()

        @pl.when(s == steps + PICK_LAG - 1)
        def _():
            lax.fori_loop(0, steps - 1, drain_rows, 0)

        @pl.when(s >= PICK_LAG)
        def _():
            row_copy(1, s - PICK_LAG).wait_recv()
            row_copy(2, s - PICK_LAG).wait_recv()
            pick(s - PICK_LAG)

        @pl.when(s == steps + 1)
        def _():
            lax.fori_loop(0, steps, drain_sums, 0)

        @pl.when(s < steps)
        def _():
            core_copy(s).wait_recv()
            to_x[s] = own[s, 0] + from_core[s, 0]
            x_copy(s).start()

        @pl.when(s == steps)
        def _():
            lax.fori_loop(0, arrivals, drain_ring, 0)

        @pl.when(jnp.logical_and(s >= SUM_LAG, s < steps + SUM_LAG))
        def _():
            before = s - SUM_LAG
            x_copy(before).wait_recv()
            total = own[before, 1] + from_core[before, 1] + from_x[before]
            for way in range(2):
                ladder[pl.ds(rows_at(before, way), piece_rows), :] = total[way * piece_rows : (way + 1) * piece_rows]
            for i in range(2 * piece_rows):
                other = partner[sector, rows_at(before, i // piece_rows) + i % piece_rows]
                mirror[pl.ds(i, 1), :] = ladder[pl.ds(other, 1), :]
            results[before, core * 2 + side] = (0.5 * (total - mirror[...])).astype(jnp.bfloat16)
            row_copy(0, before).start()
            row_copy(1, before).start()

        return carry

    lax.fori_loop(0, steps + PICK_LAG, step, 0)

    cut_rows = out_rows // FINAL_CUTS
    cuts = [pl.ds(cut * cut_rows, cut_rows) for cut in range(FINAL_CUTS)]
    outgoing = [pltpu.make_async_copy(rounded.at[at], out.at[at], out_sem.at[cut]) for cut, at in enumerate(cuts)]
    for at, copy in zip(cuts, outgoing):
        rounded[at, :] = chosen[at, :].astype(jnp.bfloat16)
        copy.start()

    for kind in range(3):
        row_copy(kind, steps - 1).wait_send()
    for copy in outgoing:
        copy.wait()


def body(amplitudes, integrals, allowed, partner):
    rows, depth = amplitudes.shape
    e_rows = integrals.shape[0]
    pieces, piece_rows, quarter = PIECES, rows // PIECES, e_rows // 4
    arrivals = pieces * (RING - 1) // 2
    steps = pieces // 2 + arrivals
    pairs = rows * RING
    out_rows = pairs // 4
    f32, bf16 = jnp.float32, jnp.bfloat16
    dma = pltpu.SemaphoreType.DMA
    anywhere = pl.BlockSpec(memory_space=pl.ANY)
    return pl.pallas_call(
        kernel,
        out_shape=jax.ShapeDtypeStruct((out_rows, e_rows), bf16),
        in_specs=[anywhere] * 4,
        out_specs=anywhere,
        scratch_shapes=[
            pltpu.SMEM(allowed.shape, jnp.int32),
            pltpu.SMEM(partner.shape, jnp.int32),
            pltpu.VMEM((RING * pieces, piece_rows, depth), bf16),
            pltpu.VMEM((e_rows, depth), bf16),
            pltpu.VMEM((steps, 2, 2 * piece_rows, quarter), f32),
            pltpu.VMEM((steps, 2, 2 * piece_rows, quarter), f32),
            pltpu.VMEM((steps, 2, 2 * piece_rows, quarter), f32),
            pltpu.VMEM((steps, 2 * piece_rows, quarter), f32),
            pltpu.VMEM((steps, 2 * piece_rows, quarter), f32),
            pltpu.VMEM((pairs, quarter), f32),
            pltpu.VMEM((2 * piece_rows, quarter), f32),
            pltpu.VMEM((steps, 4, 2 * piece_rows, quarter), bf16),
            pltpu.VMEM((out_rows, LANES), jnp.int32),
            pltpu.VMEM((out_rows, e_rows), f32),
            pltpu.VMEM((out_rows, e_rows), bf16),
            dma((4,)),
            dma((2, arrivals)),
            dma((2, arrivals)),
            dma((steps,)),
            dma((steps,)),
            dma((steps,)),
            dma((steps,)),
            dma((3, steps)),
            dma((3, steps)),
            dma((FINAL_CUTS,)),
        ],
        compiler_params=pltpu.CompilerParams(
            collective_id=0, has_side_effects=True, vmem_limit_bytes=56 * 1024 * 1024
        ),
        cost_estimate=pl.CostEstimate(
            flops=2 * pairs * e_rows * depth, bytes_accessed=2 * (e_rows * depth + rows * depth + out_rows * e_rows), transcendentals=0
        ),
        name="ladder_residual",
    )(amplitudes.reshape(pieces, piece_rows, depth), integrals, allowed, partner)


def solution(mesh):
    return jax.shard_map(
        body,
        mesh=mesh,
        in_specs=(P("blk", "col"), P("blk", "col"), P(), P()),
        out_specs=P("col", "blk"),
        check_vma=False,
    )
```

```python
import functools

import jax
import jax.numpy as jnp
from jax import lax
from jax.experimental import pallas as pl
from jax.experimental.pallas import tpu as pltpu
from jax.sharding import PartitionSpec as P

MESH = pl.DeviceIdType.MESH
RING = 8
PIECES = 4
WINDOW = 4
FINAL_CUTS = 4
GROUP = 16
LANES = 128
SUM_LAG, PASS_LAG, PICK_LAG = 1, 3, 4


def kernel(
    amplitudes, integrals, allowed_in, partner_in, out,
    allowed, partner, held, weights, own, to_core, from_core, to_x, from_x, ladder, mirror, results, partners, chosen,
    load_sem, ring_send, ring_recv, core_send, core_recv, x_send, x_recv, row_send, row_recv,
):
    pieces, piece_rows, depth = amplitudes.shape
    half = pieces // 2
    arrivals = pieces * (RING - 1) // 2
    steps = half + arrivals
    block_rows = pieces * piece_rows
    quarter = integrals.shape[0] // 4
    out_rows = out.shape[0]

    blk, col = lax.axis_index("blk"), lax.axis_index("col")
    sector, member = blk // RING, blk % RING
    side, core = col // 2, col % 2
    first = sector * RING
    right = (first + (member + 1) % RING, col)
    left = (first + (member + RING - 1) % RING, col)
    core_peer = (blk, side * 2 + 1 - core)
    x_peer = (blk, (1 - side) * 2 + core)

    load_t = pltpu.make_async_copy(amplitudes, held.at[pl.ds(0, pieces)], load_sem.at[0])
    load_v = pltpu.make_async_copy(integrals, weights, load_sem.at[1])
    load_allowed = pltpu.make_async_copy(allowed_in, allowed, load_sem.at[2])
    load_partner = pltpu.make_async_copy(partner_in, partner, load_sem.at[3])
    load_t.start()
    load_v.start()
    load_allowed.start()
    load_partner.start()

    barrier = pltpu.get_barrier_semaphore()
    for peer in (right, left, core_peer, x_peer):
        pl.semaphore_signal(barrier, inc=1, device_id=peer, device_id_type=MESH)
    pl.semaphore_wait(barrier, 4)

    def ring_copy(way, k, source=None):
        if source is None:
            start = k if way == 0 else (k + half) % pieces
            forward = pieces + 2 * (k - pieces) + way
            source = held.at[jnp.where(k < pieces, start, forward)]
        return pltpu.make_async_remote_copy(
            src_ref=source,
            dst_ref=held.at[pieces + 2 * k + way],
            send_sem=ring_send.at[way, k],
            recv_sem=ring_recv.at[way, k],
            device_id=(right, left)[way],
            device_id_type=MESH,
        )

    def row_copy(kind, s):
        place = results.at[s, core * 2 + (1 - side if kind == 2 else side)]
        return pltpu.make_async_remote_copy(
            src_ref=place, dst_ref=place, send_sem=row_send.at[kind, s], recv_sem=row_recv.at[kind, s],
            device_id=x_peer if kind == 0 else core_peer, device_id_type=MESH,
        )

    def core_copy(s):
        return pltpu.make_async_remote_copy(
            src_ref=to_core.at[s], dst_ref=from_core.at[s], send_sem=core_send.at[s], recv_sem=core_recv.at[s],
            device_id=core_peer, device_id_type=MESH,
        )

    def x_copy(s):
        return pltpu.make_async_remote_copy(
            src_ref=to_x.at[s], dst_ref=from_x.at[s], send_sem=x_send.at[s], recv_sem=x_recv.at[s],
            device_id=x_peer, device_id_type=MESH,
        )

    for k in range(WINDOW):
        ring_copy(0, k, amplitudes.at[k]).start()
        ring_copy(1, k, amplitudes.at[(k + half) % pieces]).start()

    ladder[...] = jnp.zeros_like(ladder)
    load_partner.wait()

    def spread(g, carry):
        for i in range(GROUP):
            value = partner[sector, col * out_rows + g * GROUP + i]
            partners[pl.ds(g * GROUP + i, 1), :] = jnp.full((1, LANES), value, jnp.int32)
        return carry

    lax.fori_loop(0, out_rows // GROUP, spread, 0)
    load_allowed.wait()
    load_v.wait()
    strip = 64
    width = depth // 2
    for tile in range(2):
        flag = allowed[sector, member, col * 2 + tile].astype(jnp.float32)
        factor = jnp.full((strip, width), flag, jnp.float32).astype(jnp.bfloat16)

        def mask(i, carry, tile=tile, factor=factor):
            at = (pl.ds(pl.multiple_of(i * strip, strip), strip), pl.ds(tile * width, width))
            weights[at] = weights[at] * factor
            return carry

        lax.fori_loop(0, integrals.shape[0] // strip, mask, 0)
    load_t.wait()

    def product(s, e_block):
        rows = held[pl.ds(2 * s, 2)].reshape(2 * piece_rows, depth)
        block = weights[pl.ds(pl.multiple_of(e_block * quarter, quarter), quarter), :]
        return lax.dot_general(rows, block, (((1,), (1,)), ((), ())), preferred_element_type=jnp.float32)

    def rows_at(s, way):
        t = s - half
        t_block = jnp.where(way == 0, member + RING - 1 - t // pieces, member + 1 + t // pieces) % RING
        t_piece = jnp.where(way == 0, t % pieces, (t % pieces + half) % pieces)
        block = jnp.where(s < half, member, t_block)
        piece = jnp.where(s < half, 2 * s + way, t_piece)
        return pl.multiple_of(block * block_rows + piece * piece_rows, piece_rows)

    def in_chunk(rows, s):
        first_rows, second_rows = rows_at(s, 0), rows_at(s, 1)
        return jnp.logical_or(
            jnp.logical_and(rows >= first_rows, rows < first_rows + piece_rows),
            jnp.logical_and(rows >= second_rows, rows < second_rows + piece_rows),
        )

    def pick(s):
        shape = (out_rows, 2 * piece_rows)
        mine = col * out_rows + lax.broadcasted_iota(jnp.int32, shape, 0)
        other = partners[:, : 2 * piece_rows]
        lane = lax.broadcasted_iota(jnp.int32, shape, 1)
        at_lane = jnp.where(lane < piece_rows, rows_at(s, 0) + lane, rows_at(s, 1) + lane - piece_rows)
        mine_here = in_chunk(mine, s)
        wanted = jnp.where(mine_here, mine, other)
        sign = jnp.where(mine_here, 1.0, -1.0)
        choice = jnp.where(wanted == at_lane, sign, 0.0).astype(jnp.bfloat16)
        mine_wide = col * out_rows + lax.broadcasted_iota(jnp.int32, (out_rows, LANES), 0)
        hit = jnp.logical_or(in_chunk(mine_wide, s), in_chunk(partners[...], s))
        for e_block in range(4):
            fresh = jnp.dot(choice, results[s, e_block], preferred_element_type=jnp.float32)
            for lanes in range(0, quarter, LANES):
                at = slice(e_block * quarter + lanes, e_block * quarter + lanes + LANES)
                chosen[:, at] = jnp.where(hit, fresh[:, lanes : lanes + LANES], chosen[:, at])

    def drain_ring(k, carry):
        for way in range(2):
            ring_copy(way, k).wait_send()
        return carry

    def drain_sums(s, carry):
        core_copy(s).wait_send()
        x_copy(s).wait_send()
        return carry

    def drain_rows(s, carry):
        for kind in range(3):
            row_copy(kind, s).wait_send()
        return carry

    def step(s, carry):
        @pl.when(jnp.logical_and(s >= half, s < steps))
        def _():
            t = s - half
            for way in range(2):
                ring_copy(way, t).wait_recv()

            @pl.when(t + WINDOW < arrivals)
            def _():
                for way in range(2):
                    ring_copy(way, t + WINDOW).start()

        @pl.when(s < steps)
        def _():
            to_core[s, 0] = product(s, (1 - core) * 2 + 1 - side)
            to_core[s, 1] = product(s, (1 - core) * 2 + side)
            core_copy(s).start()
            own[s, 0] = product(s, core * 2 + 1 - side)
            own[s, 1] = product(s, core * 2 + side)

        @pl.when(jnp.logical_and(s >= PASS_LAG, s < steps + PASS_LAG))
        def _():
            row_copy(0, s - PASS_LAG).wait_recv()
            row_copy(2, s - PASS_LAG).start()

        @pl.when(s == steps + PICK_LAG - 1)
        def _():
            lax.fori_loop(0, steps - 1, drain_rows, 0)

        @pl.when(s >= PICK_LAG)
        def _():
            row_copy(1, s - PICK_LAG).wait_recv()
            row_copy(2, s - PICK_LAG).wait_recv()
            pick(s - PICK_LAG)

        @pl.when(s == steps + 1)
        def _():
            lax.fori_loop(0, steps, drain_sums, 0)

        @pl.when(s < steps)
        def _():
            core_copy(s).wait_recv()
            to_x[s] = own[s, 0] + from_core[s, 0]
            x_copy(s).start()

        @pl.when(s == steps)
        def _():
            lax.fori_loop(0, arrivals, drain_ring, 0)

        @pl.when(jnp.logical_and(s >= SUM_LAG, s < steps + SUM_LAG))
        def _():
            before = s - SUM_LAG
            x_copy(before).wait_recv()
            total = own[before, 1] + from_core[before, 1] + from_x[before]
            for way in range(2):
                ladder[pl.ds(rows_at(before, way), piece_rows), :] = total[way * piece_rows : (way + 1) * piece_rows]
            for i in range(2 * piece_rows):
                other = partner[sector, rows_at(before, i // piece_rows) + i % piece_rows]
                mirror[pl.ds(i, 1), :] = ladder[pl.ds(other, 1), :]
            results[before, core * 2 + side] = (0.5 * (total - mirror[...])).astype(jnp.bfloat16)
            row_copy(0, before).start()
            row_copy(1, before).start()

        return carry

    lax.fori_loop(0, steps + PICK_LAG, step, 0)

    strip_rows = out_rows // FINAL_CUTS

    def round_strip(i, carry):
        at = pl.ds(pl.multiple_of(i * strip_rows, strip_rows), strip_rows)
        out[at, :] = chosen[at, :].astype(jnp.bfloat16)
        return carry

    lax.fori_loop(0, FINAL_CUTS, round_strip, 0)
    for kind in range(3):
        row_copy(kind, steps - 1).wait_send()


def body(amplitudes, integrals, allowed, partner):
    rows, depth = amplitudes.shape
    e_rows = integrals.shape[0]
    pieces, piece_rows, quarter = PIECES, rows // PIECES, e_rows // 4
    arrivals = pieces * (RING - 1) // 2
    steps = pieces // 2 + arrivals
    pairs = rows * RING
    out_rows = pairs // 4
    f32, bf16 = jnp.float32, jnp.bfloat16
    dma = pltpu.SemaphoreType.DMA
    anywhere = pl.BlockSpec(memory_space=pl.ANY)
    return pl.pallas_call(
        kernel,
        out_shape=pltpu.VMEM((out_rows, e_rows), bf16),
        in_specs=[anywhere] * 4,
        out_specs=pl.BlockSpec(memory_space=pltpu.VMEM),
        scratch_shapes=[
            pltpu.SMEM(allowed.shape, jnp.int32),
            pltpu.SMEM(partner.shape, jnp.int32),
            pltpu.VMEM((RING * pieces, piece_rows, depth), bf16),
            pltpu.VMEM((e_rows, depth), bf16),
            pltpu.VMEM((steps, 2, 2 * piece_rows, quarter), f32),
            pltpu.VMEM((steps, 2, 2 * piece_rows, quarter), f32),
            pltpu.VMEM((steps, 2, 2 * piece_rows, quarter), f32),
            pltpu.VMEM((steps, 2 * piece_rows, quarter), f32),
            pltpu.VMEM((steps, 2 * piece_rows, quarter), f32),
            pltpu.VMEM((pairs, quarter), f32),
            pltpu.VMEM((2 * piece_rows, quarter), f32),
            pltpu.VMEM((steps, 4, 2 * piece_rows, quarter), bf16),
            pltpu.VMEM((out_rows, LANES), jnp.int32),
            pltpu.VMEM((out_rows, e_rows), f32),
            dma((4,)),
            dma((2, arrivals)),
            dma((2, arrivals)),
            dma((steps,)),
            dma((steps,)),
            dma((steps,)),
            dma((steps,)),
            dma((3, steps)),
            dma((3, steps)),
        ],
        compiler_params=pltpu.CompilerParams(
            collective_id=0, has_side_effects=True, vmem_limit_bytes=56 * 1024 * 1024
        ),
        cost_estimate=pl.CostEstimate(
            flops=2 * pairs * e_rows * depth, bytes_accessed=2 * (e_rows * depth + rows * depth + out_rows * e_rows), transcendentals=0
        ),
        name="ladder_residual",
    )(amplitudes.reshape(pieces, piece_rows, depth), integrals, allowed, partner)


def solution(mesh):
    return jax.shard_map(
        body,
        mesh=mesh,
        in_specs=(P("blk", "col"), P("blk", "col"), P(), P()),
        out_specs=P("col", "blk"),
        check_vma=False,
    )
```

```python
import functools

import jax
import jax.numpy as jnp
from jax import lax
from jax.experimental import pallas as pl
from jax.experimental.pallas import tpu as pltpu
from jax.sharding import PartitionSpec as P

MESH = pl.DeviceIdType.MESH
RING = 8
PIECES = 4
WINDOW = 4
FINAL_CUTS = 4
GROUP = 16
LANES = 128
SUM_LAG, PASS_LAG, PICK_LAG = 1, 3, 4


def kernel(
    amplitudes, integrals, allowed_in, partner_in, out,
    allowed, partner, held, weights, own, to_core, from_core, to_x, from_x, ladder, mirror, results, partners, chosen,
    load_sem, ring_send, ring_recv, core_send, core_recv, x_send, x_recv, row_send, row_recv,
):
    pieces, piece_rows, depth = amplitudes.shape
    half = pieces // 2
    arrivals = pieces * (RING - 1) // 2
    steps = half + arrivals
    block_rows = pieces * piece_rows
    quarter = integrals.shape[0] // 4
    out_rows = out.shape[0]

    blk, col = lax.axis_index("blk"), lax.axis_index("col")
    sector, member = blk // RING, blk % RING
    side, core = col // 2, col % 2
    first = sector * RING
    right = (first + (member + 1) % RING, col)
    left = (first + (member + RING - 1) % RING, col)
    core_peer = (blk, side * 2 + 1 - core)
    x_peer = (blk, (1 - side) * 2 + core)

    load_t = pltpu.make_async_copy(amplitudes, held.at[pl.ds(0, pieces)], load_sem.at[0])
    load_v = pltpu.make_async_copy(integrals, weights, load_sem.at[1])
    load_allowed = pltpu.make_async_copy(allowed_in, allowed, load_sem.at[2])
    load_partner = pltpu.make_async_copy(partner_in, partner, load_sem.at[3])
    load_t.start()
    load_v.start()
    load_allowed.start()
    load_partner.start()

    barrier = pltpu.get_barrier_semaphore()
    for peer in (right, left, core_peer, x_peer):
        pl.semaphore_signal(barrier, inc=1, device_id=peer, device_id_type=MESH)
    pl.semaphore_wait(barrier, 4)

    def ring_copy(way, k, source=None):
        if source is None:
            start = k if way == 0 else (k + half) % pieces
            forward = pieces + 2 * (k - pieces) + way
            source = held.at[jnp.where(k < pieces, start, forward)]
        return pltpu.make_async_remote_copy(
            src_ref=source,
            dst_ref=held.at[pieces + 2 * k + way],
            send_sem=ring_send.at[way, k],
            recv_sem=ring_recv.at[way, k],
            device_id=(right, left)[way],
            device_id_type=MESH,
        )

    def row_copy(kind, s):
        place = results.at[s, core * 2 + side] if kind == 0 else results.at[s, pl.ds(core * 2, 2)]
        return pltpu.make_async_remote_copy(
            src_ref=place, dst_ref=place, send_sem=row_send.at[kind, s], recv_sem=row_recv.at[kind, s],
            device_id=x_peer if kind == 0 else core_peer, device_id_type=MESH,
        )

    def core_copy(s):
        return pltpu.make_async_remote_copy(
            src_ref=to_core.at[s], dst_ref=from_core.at[s], send_sem=core_send.at[s], recv_sem=core_recv.at[s],
            device_id=core_peer, device_id_type=MESH,
        )

    def x_copy(s):
        return pltpu.make_async_remote_copy(
            src_ref=to_x.at[s], dst_ref=from_x.at[s], send_sem=x_send.at[s], recv_sem=x_recv.at[s],
            device_id=x_peer, device_id_type=MESH,
        )

    for k in range(WINDOW):
        ring_copy(0, k, amplitudes.at[k]).start()
        ring_copy(1, k, amplitudes.at[(k + half) % pieces]).start()

    ladder[...] = jnp.zeros_like(ladder)
    load_partner.wait()

    def spread(g, carry):
        for i in range(GROUP):
            value = partner[sector, col * out_rows + g * GROUP + i]
            partners[pl.ds(g * GROUP + i, 1), :] = jnp.full((1, LANES), value, jnp.int32)
        return carry

    lax.fori_loop(0, out_rows // GROUP, spread, 0)
    load_allowed.wait()
    load_v.wait()
    strip = 64
    width = depth // 2
    for tile in range(2):
        flag = allowed[sector, member, col * 2 + tile].astype(jnp.float32)
        factor = jnp.full((strip, width), flag, jnp.float32).astype(jnp.bfloat16)

        def mask(i, carry, tile=tile, factor=factor):
            at = (pl.ds(pl.multiple_of(i * strip, strip), strip), pl.ds(tile * width, width))
            weights[at] = weights[at] * factor
            return carry

        lax.fori_loop(0, integrals.shape[0] // strip, mask, 0)
    load_t.wait()

    def product(s, e_block):
        rows = held[pl.ds(2 * s, 2)].reshape(2 * piece_rows, depth)
        block = weights[pl.ds(pl.multiple_of(e_block * quarter, quarter), quarter), :]
        return lax.dot_general(rows, block, (((1,), (1,)), ((), ())), preferred_element_type=jnp.float32)

    def rows_at(s, way):
        t = s - half
        t_block = jnp.where(way == 0, member + RING - 1 - t // pieces, member + 1 + t // pieces) % RING
        t_piece = jnp.where(way == 0, t % pieces, (t % pieces + half) % pieces)
        block = jnp.where(s < half, member, t_block)
        piece = jnp.where(s < half, 2 * s + way, t_piece)
        return pl.multiple_of(block * block_rows + piece * piece_rows, piece_rows)

    def in_chunk(rows, s):
        first_rows, second_rows = rows_at(s, 0), rows_at(s, 1)
        return jnp.logical_or(
            jnp.logical_and(rows >= first_rows, rows < first_rows + piece_rows),
            jnp.logical_and(rows >= second_rows, rows < second_rows + piece_rows),
        )

    def pick(s):
        shape = (out_rows, 2 * piece_rows)
        mine = col * out_rows + lax.broadcasted_iota(jnp.int32, shape, 0)
        other = partners[:, : 2 * piece_rows]
        lane = lax.broadcasted_iota(jnp.int32, shape, 1)
        at_lane = jnp.where(lane < piece_rows, rows_at(s, 0) + lane, rows_at(s, 1) + lane - piece_rows)
        mine_here = in_chunk(mine, s)
        wanted = jnp.where(mine_here, mine, other)
        sign = jnp.where(mine_here, 1.0, -1.0)
        choice = jnp.where(wanted == at_lane, sign, 0.0).astype(jnp.bfloat16)
        mine_wide = col * out_rows + lax.broadcasted_iota(jnp.int32, (out_rows, LANES), 0)
        hit = jnp.logical_or(in_chunk(mine_wide, s), in_chunk(partners[...], s))
        for e_block in range(4):
            fresh = jnp.dot(choice, results[s, e_block], preferred_element_type=jnp.float32)
            for lanes in range(0, quarter, LANES):
                at = slice(e_block * quarter + lanes, e_block * quarter + lanes + LANES)
                chosen[:, at] = jnp.where(hit, fresh[:, lanes : lanes + LANES], chosen[:, at])

    def drain_ring(k, carry):
        for way in range(2):
            ring_copy(way, k).wait_send()
        return carry

    def drain_sums(s, carry):
        core_copy(s).wait_send()
        x_copy(s).wait_send()
        return carry

    def drain_rows(s, carry):
        for kind in range(2):
            row_copy(kind, s).wait_send()
        return carry

    def step(s, carry):
        @pl.when(jnp.logical_and(s >= half, s < steps))
        def _():
            t = s - half
            for way in range(2):
                ring_copy(way, t).wait_recv()

            @pl.when(t + WINDOW < arrivals)
            def _():
                for way in range(2):
                    ring_copy(way, t + WINDOW).start()

        @pl.when(s < steps)
        def _():
            to_core[s, 0] = product(s, (1 - core) * 2 + 1 - side)
            to_core[s, 1] = product(s, (1 - core) * 2 + side)
            core_copy(s).start()
            own[s, 0] = product(s, core * 2 + 1 - side)
            own[s, 1] = product(s, core * 2 + side)

        @pl.when(jnp.logical_and(s >= PASS_LAG, s < steps + PASS_LAG))
        def _():
            row_copy(0, s - PASS_LAG).wait_recv()
            row_copy(1, s - PASS_LAG).start()

        @pl.when(s == steps + PICK_LAG - 1)
        def _():
            lax.fori_loop(0, steps - 1, drain_rows, 0)

        @pl.when(s >= PICK_LAG)
        def _():
            row_copy(1, s - PICK_LAG).wait_recv()
            pick(s - PICK_LAG)

        @pl.when(s == steps + 1)
        def _():
            lax.fori_loop(0, steps, drain_sums, 0)

        @pl.when(s < steps)
        def _():
            core_copy(s).wait_recv()
            to_x[s] = own[s, 0] + from_core[s, 0]
            x_copy(s).start()

        @pl.when(s == steps)
        def _():
            lax.fori_loop(0, arrivals, drain_ring, 0)

        @pl.when(jnp.logical_and(s >= SUM_LAG, s < steps + SUM_LAG))
        def _():
            before = s - SUM_LAG
            x_copy(before).wait_recv()
            total = own[before, 1] + from_core[before, 1] + from_x[before]
            for way in range(2):
                ladder[pl.ds(rows_at(before, way), piece_rows), :] = total[way * piece_rows : (way + 1) * piece_rows]
            for i in range(2 * piece_rows):
                other = partner[sector, rows_at(before, i // piece_rows) + i % piece_rows]
                mirror[pl.ds(i, 1), :] = ladder[pl.ds(other, 1), :]
            results[before, core * 2 + side] = (0.5 * (total - mirror[...])).astype(jnp.bfloat16)
            row_copy(0, before).start()

        return carry

    lax.fori_loop(0, steps + PICK_LAG, step, 0)

    strip_rows = out_rows // FINAL_CUTS

    def round_strip(i, carry):
        at = pl.ds(pl.multiple_of(i * strip_rows, strip_rows), strip_rows)
        out[at, :] = chosen[at, :].astype(jnp.bfloat16)
        return carry

    lax.fori_loop(0, FINAL_CUTS, round_strip, 0)
    for kind in range(2):
        row_copy(kind, steps - 1).wait_send()


def body(amplitudes, integrals, allowed, partner):
    rows, depth = amplitudes.shape
    e_rows = integrals.shape[0]
    pieces, piece_rows, quarter = PIECES, rows // PIECES, e_rows // 4
    arrivals = pieces * (RING - 1) // 2
    steps = pieces // 2 + arrivals
    pairs = rows * RING
    out_rows = pairs // 4
    f32, bf16 = jnp.float32, jnp.bfloat16
    dma = pltpu.SemaphoreType.DMA
    anywhere = pl.BlockSpec(memory_space=pl.ANY)
    return pl.pallas_call(
        kernel,
        out_shape=pltpu.VMEM((out_rows, e_rows), bf16),
        in_specs=[anywhere] * 4,
        out_specs=pl.BlockSpec(memory_space=pltpu.VMEM),
        scratch_shapes=[
            pltpu.SMEM(allowed.shape, jnp.int32),
            pltpu.SMEM(partner.shape, jnp.int32),
            pltpu.VMEM((RING * pieces, piece_rows, depth), bf16),
            pltpu.VMEM((e_rows, depth), bf16),
            pltpu.VMEM((steps, 2, 2 * piece_rows, quarter), f32),
            pltpu.VMEM((steps, 2, 2 * piece_rows, quarter), f32),
            pltpu.VMEM((steps, 2, 2 * piece_rows, quarter), f32),
            pltpu.VMEM((steps, 2 * piece_rows, quarter), f32),
            pltpu.VMEM((steps, 2 * piece_rows, quarter), f32),
            pltpu.VMEM((pairs, quarter), f32),
            pltpu.VMEM((2 * piece_rows, quarter), f32),
            pltpu.VMEM((steps, 4, 2 * piece_rows, quarter), bf16),
            pltpu.VMEM((out_rows, LANES), jnp.int32),
            pltpu.VMEM((out_rows, e_rows), f32),
            dma((4,)),
            dma((2, arrivals)),
            dma((2, arrivals)),
            dma((steps,)),
            dma((steps,)),
            dma((steps,)),
            dma((steps,)),
            dma((2, steps)),
            dma((2, steps)),
        ],
        compiler_params=pltpu.CompilerParams(
            collective_id=0, has_side_effects=True, vmem_limit_bytes=56 * 1024 * 1024
        ),
        cost_estimate=pl.CostEstimate(
            flops=2 * pairs * e_rows * depth, bytes_accessed=2 * (e_rows * depth + rows * depth + out_rows * e_rows), transcendentals=0
        ),
        name="ladder_residual",
    )(amplitudes.reshape(pieces, piece_rows, depth), integrals, allowed, partner)


def solution(mesh):
    return jax.shard_map(
        body,
        mesh=mesh,
        in_specs=(P("blk", "col"), P("blk", "col"), P(), P()),
        out_specs=P("col", "blk"),
        check_vma=False,
    )
```
